32 devices in a mesh: outer: 2 (over x), sec: 8 (over z, core), tp: 2 (over y).
Axes of the slice: x: 2, y: 2, z: 4, core: 2. Of those that a mesh axis runs over, the one named last changes fastest.
Arguments:
- tile_maps: bfloat16 [32, 12, 12, 3072], P(('outer', 'sec'), None, None, 'tp'), may hold values from -6 to 6
- tile_shape: int32 [32, 2], P(('outer', 'sec')), may hold values from 4 to 12
- conv_kernel: float32 [7, 7, 3072], P(None, None, 'tp'), may hold values from -0.875 to 0.875
- norm_gain: float32 [3072], P('tp'), may hold values from 0.25 to 1.75
- norm_bias: float32 [3072], P('tp'), may hold values from -3 to 3
- projector: bfloat16 [3072, 7168], P('tp', 'sec'), may hold values from -0.109375 to 0.109375
- text_rows: bfloat16 [9216, 7168], P(('outer', 'sec'), 'tp'), may hold values from -6 to 6
- row_order: int32 [16, 576], P(('outer', 'sec')), may hold values from 0 to 575, each once within a row
- seq_gain: float32 [7168], P('tp'), may hold values from 0.25 to 1.75
- cotangent: bfloat16 [9216, 7168], P(('outer', 'sec'), 'tp'), may hold values from -0.2772166 to 0.2772166, as said below
Outputs:
- normed: bfloat16 [9216, 7168], P(('outer', 'sec'), 'tp')
- kernel_delta: float32 [7, 7, 3072], P(None, None, 'tp')
- gain_delta: float32 [3072], P('tp')
- bias_delta: float32 [3072], P('tp')
The draws below stay inside these ranges and needn't reach their ends.
Inputs may be any that keep to these rules, and one draw needn't show every extreme that they name: `row_order`: each row lists where the visual tokens arriving at that device stand, in arrival order, then the text rows. `tile_shape`: valid rows and columns of each tile, the rest of the map is padding. `cotangent`: gradient of the training loss.
All inputs are finite; a program needn't handle non-finite values.
Results may differ from the reference program's by a relative error of at most 0.0043.
Values may be sent and summed in bfloat16 or wider, within the bound.
A program may use at most 128 MiB of HBM per device.

```python
import math
import jax
import jax.numpy as jnp
from jax import lax

C = 3072
D = 7168
GRID = 12
TILES_DEV = 2
ROWS_DEV = 288
SEQ_DEV = 576
N_OUTER = 2
N_SEC = 8


def draw_cotangent(key, part):
    row_count = N_OUTER * N_SEC * SEQ_DEV
    overall = math.sqrt(20.0 * C / (ROWS_DEV * N_SEC * D))
    value_key = jax.random.fold_in(key, 11)
    low_pod = jax.random.randint(jax.random.fold_in(key, 23), (), 0, N_OUTER)
    pod_index = jnp.arange(row_count, dtype=jnp.int32) // (N_SEC * SEQ_DEV)
    factors = overall * jnp.where(pod_index == low_pod, 0.125, 1.0).astype(jnp.float32)
    values = jnp.clip(jax.random.normal(value_key, (row_count, D), jnp.float32), -4.5, 4.5)
    return (values * factors[:, None]).astype(jnp.bfloat16)


def place_ends(array, own_key, smallest, top_value):
    shape = array.shape
    spot = [jax.random.randint(jax.random.fold_in(own_key, axis), (), 0, shape[axis]) for axis in range(len(shape))]
    array = array.at[tuple(spot)].set(smallest)
    longest = shape.index(max(shape))
    spot[longest] = (spot[longest] + 1) % shape[longest]
    return array.at[tuple(spot)].set(top_value)


def block_scale(stream_key, extent, cuts, low, high):
    factor_of, own = 1.0, jax.random.fold_in(stream_key, 6)
    for axis_at, blocks in cuts:
        heights = jnp.exp(jax.random.uniform(jax.random.fold_in(own, axis_at), (blocks,), jnp.float32, low / len(cuts), high / len(cuts)))
        factor_of = factor_of * jnp.repeat(heights, extent[axis_at] // blocks).reshape([-1 if axis == axis_at else 1 for axis in range(len(extent))])
    return factor_of


def normal_values(rng, extent, scale, reach, split=(), kind=jnp.bfloat16):
    factor_of = block_scale(rng, extent, split, -0.22, 0.18) if split else 1.0
    values = jax.random.normal(rng, extent, jnp.float32) * scale * factor_of
    return jnp.minimum(jnp.maximum(values, -reach), reach).astype(kind)


def setup_inputs(seed: int = 0) -> dict:
    key_list = jax.random.split(jax.random.key(seed), 11)
    tile_maps = normal_values(key_list[0], (N_OUTER * N_SEC * TILES_DEV, GRID, GRID, C), 1.0, 6.0, ((0, 16), (3, 2)))
    tile_shape = place_ends(jax.random.randint(key_list[1], (N_OUTER * N_SEC * TILES_DEV, 2), 4, GRID + 1), jax.random.fold_in(key_list[1], 1), 4, GRID).astype(jnp.int32)
    conv_kernel = normal_values(key_list[2], (7, 7, C), 49 ** -0.5, 0.875, ((2, 2),), jnp.float32)
    norm_gain = jnp.clip(1.0 + 0.15 * jax.random.normal(key_list[3], (C,), jnp.float32), 0.25, 1.75)
    norm_bias = normal_values(key_list[4], (C,), 0.5, 3.0, ((0, 2),), jnp.float32)
    projector = normal_values(key_list[5], (C, D), C ** -0.5, 0.109375, ((0, 2), (1, 8)))
    text_rows = normal_values(key_list[6], (N_OUTER * N_SEC * SEQ_DEV, D), 1.0, 6.0, ((0, 16), (1, 2)))
    row_order = jax.vmap(lambda own: jax.random.permutation(own, SEQ_DEV))(jax.random.split(key_list[7], (N_OUTER * N_SEC))).reshape((N_OUTER * N_SEC, SEQ_DEV)).astype(jnp.int32)
    seq_gain = jnp.clip(1.0 + 0.15 * jax.random.normal(key_list[8], (D,), jnp.float32), 0.25, 1.75)
    cotangent = draw_cotangent(jax.random.fold_in(key_list[10], 71), 0)
    return {"tile_maps": tile_maps, "tile_shape": tile_shape, "conv_kernel": conv_kernel, "norm_gain": norm_gain, "norm_bias": norm_bias, "projector": projector, "text_rows": text_rows, "row_order": row_order, "seq_gain": seq_gain, "cotangent": cotangent}


def shape_mask(tile_shape):
    places = jnp.arange(GRID, dtype=jnp.int32)
    rows_ok = places[None, :] < tile_shape[:, 0:1]
    cols_ok = places[None, :] < tile_shape[:, 1:2]
    return (rows_ok[:, :, None] & cols_ok[:, None, :]).astype(jnp.float32)

def reference(tile_maps, tile_shape, conv_kernel, norm_gain, norm_bias, projector, text_rows, row_order, seq_gain, cotangent):
    validity = shape_mask(tile_shape)[..., None]
    masked = tile_maps.astype(jnp.float32) * validity
    padded = jnp.pad(masked, ((0, 0), (3, 3), (3, 3), (0, 0)))
    conv_out = jnp.zeros(masked.shape, jnp.float32)
    for row_off in range(7):
        for col_off in range(7):
            conv_out = conv_out + padded[:, row_off:row_off + GRID, col_off:col_off + GRID, :] * conv_kernel[row_off, col_off]
    center = lax.optimization_barrier(jnp.mean(conv_out, axis=-1, keepdims=True))
    second = lax.optimization_barrier(jnp.mean(conv_out * conv_out, axis=-1, keepdims=True))
    inverse = lax.rsqrt(second - center * center + 1e-06)
    normal = (conv_out - center) * inverse
    features = (validity * (normal * norm_gain + norm_bias)).astype(jnp.bfloat16)
    visual = jnp.dot(features.reshape(-1, C), projector, preferred_element_type=jnp.float32).astype(jnp.bfloat16)
    groups = N_OUTER * N_SEC
    share = ROWS_DEV // N_SEC
    routed = visual.reshape(N_OUTER, N_SEC, N_SEC, share, D).transpose(0, 2, 1, 3, 4).reshape(groups, ROWS_DEV, D)
    sequence = text_rows.reshape(groups, SEQ_DEV, D)
    positions = row_order[:, :ROWS_DEV].astype(jnp.int32)
    merged = jax.vmap(lambda block, where, rows: block.at[where].set(rows))(sequence, positions, routed)
    wide = merged.astype(jnp.float32)
    inv_rms = lax.rsqrt(lax.optimization_barrier(jnp.mean(wide * wide, axis=-1, keepdims=True)) + 1e-05)
    normed = (wide * inv_rms * seq_gain).astype(jnp.bfloat16)
    upstream = cotangent.reshape(groups, SEQ_DEV, D).astype(jnp.float32) * seq_gain
    along = lax.optimization_barrier(jnp.sum(upstream * wide, axis=-1, keepdims=True))
    grad_seq = inv_rms * upstream - wide * (inv_rms * inv_rms * inv_rms) * along / D
    picked = jax.vmap(lambda block, where: block[where])(grad_seq, positions).astype(jnp.bfloat16)
    returned = picked.reshape(N_OUTER, N_SEC, N_SEC, share, D).transpose(0, 2, 1, 3, 4).reshape(-1, D)
    grad_features = jnp.dot(returned, projector.T, preferred_element_type=jnp.float32).reshape(masked.shape)
    masked_grad = grad_features * validity
    scaled = masked_grad * norm_gain
    first_mean = lax.optimization_barrier(jnp.mean(scaled, axis=-1, keepdims=True))
    second_mean = lax.optimization_barrier(jnp.mean(scaled * normal, axis=-1, keepdims=True))
    grad_conv = inverse * (scaled - first_mean - normal * second_mean)
    pod_tiles = N_SEC * TILES_DEV
    padded_pod = padded.reshape(N_OUTER, pod_tiles, GRID + 6, GRID + 6, C)
    grad_pod = grad_conv.reshape(N_OUTER, pod_tiles, GRID, GRID, C)
    kernel_rows = []
    for row_off in range(7):
        for col_off in range(7):
            window = padded_pod[:, :, row_off:row_off + GRID, col_off:col_off + GRID, :]
            kernel_rows.append(lax.optimization_barrier(jnp.sum(window * grad_pod, axis=(1, 2, 3))))
    kernel_grad = jnp.stack(kernel_rows, axis=1)
    gain_grad = lax.optimization_barrier(jnp.sum((masked_grad * normal).reshape(N_OUTER, -1, C), axis=1))
    bias_grad = lax.optimization_barrier(jnp.sum(masked_grad.reshape(N_OUTER, -1, C), axis=1))
    delta = jnp.concatenate([kernel_grad, gain_grad[:, None, :], bias_grad[:, None, :]], axis=1)
    mean_sq = lax.optimization_barrier(jnp.sum(delta * delta, axis=(1, 2))) / (51 * C)
    factor = jnp.minimum(1.0, 1.0 / jnp.sqrt(mean_sq + 1e-06))
    average = lax.optimization_barrier(jnp.mean(delta * factor[:, None, None], axis=0))
    return (normed.reshape(-1, D), average[:49].reshape(7, 7, C), average[49], average[50])
```

```python
import jax
import jax.numpy as jnp
from jax import lax
from jax.sharding import PartitionSpec as P


def shape_mask(tile_shape, grid):
    places = lax.broadcasted_iota(jnp.int32, (1, grid), 1)
    rows_ok = places < tile_shape[:, 0:1]
    cols_ok = places < tile_shape[:, 1:2]
    return (rows_ok[:, :, None] & cols_ok[:, None, :]).astype(jnp.float32)


def on_device(
    tile_maps,
    tile_shape,
    conv_kernel,
    norm_gain,
    norm_bias,
    projector,
    text_rows,
    row_order,
    seq_gain,
    cotangent,
):
    grid = tile_maps.shape[1]
    half_ch = tile_maps.shape[3]
    channels = half_ch * lax.axis_size("tp")
    rows_dev = tile_maps.shape[0] * grid * grid
    width = text_rows.shape[1] * lax.axis_size("tp")
    validity = shape_mask(tile_shape, grid)[..., None]
    masked = tile_maps.astype(jnp.float32) * validity
    padded = jnp.pad(masked, ((0, 0), (3, 3), (3, 3), (0, 0)))
    conv_out = jnp.zeros(masked.shape, jnp.float32)
    for row_off in range(7):
        for col_off in range(7):
            conv_out = (
                conv_out
                + padded[:, row_off : row_off + grid, col_off : col_off + grid, :]
                * conv_kernel[row_off, col_off]
            )
    total_one, total_two = lax.psum(
        (jnp.sum(conv_out, axis=-1), jnp.sum(conv_out * conv_out, axis=-1)), "tp"
    )
    center = (total_one / channels)[..., None]
    inverse = lax.rsqrt((total_two / channels)[..., None] - center * center + 1e-06)
    normal = (conv_out - center) * inverse
    features = (
        (validity * (normal * norm_gain + norm_bias))
        .astype(jnp.bfloat16)
        .reshape(rows_dev, half_ch)
    )
    tp_size = lax.axis_size("tp")
    half_width = text_rows.shape[1]
    mine = lax.axis_index("tp")
    swap = [(i, (i + 1) % tp_size) for i in range(tp_size)]
    gathered = lax.all_gather(projector, "sec", axis=0, tiled=False)
    per_half = gathered.shape[0] // tp_size
    own_weight = lax.dynamic_slice_in_dim(gathered, mine * per_half, per_half, axis=0)
    far_weight = lax.dynamic_slice_in_dim(gathered, (1 - mine) * per_half, per_half, axis=0)
    routed = lax.all_to_all(features, "sec", split_axis=0, concat_axis=0, tiled=True)

    def project(rows, weight):
        return jnp.concatenate(
            [
                jnp.dot(rows, weight[block], preferred_element_type=jnp.float32)
                for block in range(per_half)
            ],
            axis=1,
        )

    sent = project(routed, far_weight).astype(jnp.bfloat16)
    other = lax.ppermute(sent, "tp", swap)
    arrived = (project(routed, own_weight) + other.astype(jnp.float32)).astype(jnp.bfloat16)
    positions = row_order[0, :rows_dev]
    merged = text_rows.at[positions].set(arrived)
    wide = merged.astype(jnp.float32)
    upstream = cotangent.astype(jnp.float32) * seq_gain
    square_sum, along = lax.psum(
        (jnp.sum(wide * wide, axis=-1), jnp.sum(upstream * wide, axis=-1)), "tp"
    )
    inv_rms = lax.rsqrt(square_sum / width + 1e-05)[:, None]
    normed = (wide * inv_rms * seq_gain).astype(jnp.bfloat16)
    grad_seq = inv_rms * upstream - wide * (inv_rms * inv_rms * inv_rms) * along[:, None] / width
    picked = grad_seq[positions].astype(jnp.bfloat16)
    far_picked = lax.ppermute(picked, "tp", swap)

    def project_back(rows, weight):
        step = weight.shape[2]
        total = jnp.zeros((rows.shape[0], half_ch), jnp.float32)
        for block in range(per_half):
            total = total + lax.dot_general(
                rows[:, block * step : (block + 1) * step],
                weight[block],
                (((1,), (1,)), ((), ())),
                preferred_element_type=jnp.float32,
            )
        return total

    back = (project_back(picked, own_weight) + project_back(far_picked, far_weight)).astype(
        jnp.bfloat16
    )
    grad_rows = lax.all_to_all(back, "sec", split_axis=0, concat_axis=0, tiled=True).astype(
        jnp.float32
    )
    masked_grad = grad_rows.reshape(masked.shape) * validity
    scaled = masked_grad * norm_gain
    first_sum, second_sum = lax.psum(
        (jnp.sum(scaled, axis=-1), jnp.sum(scaled * normal, axis=-1)), "tp"
    )
    grad_conv = inverse * (
        scaled - (first_sum / channels)[..., None] - normal * (second_sum / channels)[..., None]
    )
    kernel_rows = []
    for row_off in range(7):
        for col_off in range(7):
            window = padded[:, row_off : row_off + grid, col_off : col_off + grid, :]
            kernel_rows.append(jnp.sum(window * grad_conv, axis=(0, 1, 2)))
    gain_grad = jnp.sum(masked_grad * normal, axis=(0, 1, 2))
    bias_grad = jnp.sum(masked_grad, axis=(0, 1, 2))
    local_delta = jnp.stack(kernel_rows + [gain_grad, bias_grad], axis=0)
    pods = lax.axis_size("outer")
    entries = 51 * channels
    pod_sum = lax.psum(local_delta, "sec")
    norm_sq = lax.psum(jnp.sum(pod_sum * pod_sum), "tp")
    factor = jnp.minimum(1.0, 1.0 / jnp.sqrt(norm_sq / entries + 1e-06))
    average = lax.psum(pod_sum * factor, "outer") / pods
    return (normed, average[:49].reshape(7, 7, half_ch), average[49], average[50])


def solution(mesh):
    in_specs = (
        P(("outer", "sec"), None, None, "tp"),
        P(("outer", "sec"), None),
        P(None, None, "tp"),
        P("tp"),
        P("tp"),
        P("tp", "sec"),
        P(("outer", "sec"), "tp"),
        P(("outer", "sec"), None),
        P("tp"),
        P(("outer", "sec"), "tp"),
    )
    out_specs = (P(("outer", "sec"), "tp"), P(None, None, "tp"), P("tp"), P("tp"))
    return jax.shard_map(
        on_device, mesh=mesh, in_specs=in_specs, out_specs=out_specs, check_vma=False
    )
```

```python
import jax
import jax.numpy as jnp
from jax import lax
from jax.experimental import pallas as pl
from jax.experimental.pallas import tpu as pltpu
from jax.sharding import PartitionSpec as P
import functools

MESH = pl.DeviceIdType.MESH


def gather_kernel(
    n_sec, pieces, own_ref, left_ref, right_ref, tie_ref, out_ref,
    near_sem, z_send, z_recv, x_send, x_recv, c_send, c_recv, cx_send, cx_recv,
):
    chips = n_sec // 2
    pod = lax.axis_index("outer")
    sec = lax.axis_index("sec")
    tp = lax.axis_index("tp")
    core = sec % 2
    chip = sec // 2
    half = own_ref.shape[0] // 2
    rows = half // pieces
    right_ok = chip + 1 < chips
    left_ok = chip >= 1

    barrier = pltpu.get_barrier_semaphore()

    def greet(to_pod, to_sec):
        pl.semaphore_signal(barrier, inc=1, device_id=(to_pod, to_sec, tp), device_id_type=MESH)

    greet(1 - pod, sec)
    greet(pod, 2 * chip + 1 - core)
    pl.when(right_ok)(lambda: greet(pod, sec + 2))
    pl.when(left_ok)(lambda: greet(pod, sec - 2))
    pl.semaphore_wait(barrier, 2 + right_ok.astype(jnp.int32) + left_ok.astype(jnp.int32))

    def span(part, k):
        return pl.ds(pl.multiple_of(part * half + k * rows, rows), rows)

    def place(unit, on_core, part, k):
        return out_ref.at[2 * unit + on_core, span(part, k)]

    def source(unit, side, d, k):
        if d > 1:
            return place(unit, core, pod, k)
        ref = left_ref if side == 0 else right_ref
        return ref.at[pl.ds(k * rows, rows)]

    def remote(src, dst, send, recv, to_pod, to_sec):
        return pltpu.make_async_remote_copy(
            src_ref=src, dst_ref=dst, send_sem=send, recv_sem=recv,
            device_id=(to_pod, to_sec, tp), device_id_type=MESH,
        )

    def z_copy(unit, side, d, k):
        return remote(
            source(unit, side, d, k), place(unit, core, pod, k),
            z_send.at[unit, k], z_recv.at[unit, k],
            pod, sec + 2 if side == 0 else sec - 2,
        )

    def x_copy(unit, side, d, k):
        return remote(
            source(unit, side, d, k), place(unit, core, pod, k),
            x_send.at[unit, k], x_recv.at[unit, k], 1 - pod, sec,
        )

    def c_copy(unit, side, d, k):
        return remote(
            source(unit, side, d, k), place(unit, core, pod, k),
            c_send.at[unit, k], c_recv.at[unit, k], pod, 2 * chip + 1 - core,
        )

    def cx_copy(unit, k):
        return remote(
            place(unit, core, 1 - pod, k), place(unit, core, 1 - pod, k),
            cx_send.at[unit, k], cx_recv.at[unit, k], pod, 2 * chip + 1 - core,
        )

    own_core = remote(
        own_ref, out_ref.at[sec], c_send.at[chip, 0], c_recv.at[chip, 0],
        pod, 2 * chip + 1 - core,
    )
    own_local = pltpu.make_async_copy(own_ref, out_ref.at[sec], near_sem.at[0])

    def near_copy(side):
        unit = chip - 1 if side == 0 else chip + 1
        ref = left_ref if side == 0 else right_ref
        return pltpu.make_async_copy(
            ref,
            out_ref.at[2 * unit + core, pl.ds(pl.multiple_of(pod * half, half), half)],
            near_sem.at[1 + side],
        )

    def unit_of(side, d):
        unit = chip - d if side == 0 else chip + d
        valid = unit >= 0 if side == 0 else unit < chips
        onward = jnp.logical_and(valid, right_ok if side == 0 else left_ok)
        return unit, valid, onward

    def take_x(d, k):
        for side in (0, 1):
            unit, valid, _ = unit_of(side, d)

            @pl.when(valid)
            def _():
                x_copy(unit, side, d, k).wait_recv()
                cx_copy(unit, k).start()

    for d in range(1, chips):
        for k in range(pieces):
            for side in (0, 1):
                unit, valid, onward = unit_of(side, d)

                @pl.when(valid)
                def _():
                    if d > 1:
                        z_copy(unit, side, d, k).wait_recv()

                @pl.when(onward)
                def _():
                    z_copy(unit, side, d, k).start()

                @pl.when(valid)
                def _():
                    x_copy(unit, side, d, k).start()
                    c_copy(unit, side, d, k).start()

            if d > 1:
                take_x(d - 1, k)
        if d == 1:
            own_core.start()
            own_local.start()
            for side in (0, 1):
                pl.when(unit_of(side, 1)[1])(lambda side=side: near_copy(side).start())
    for k in range(pieces):
        take_x(chips - 1, k)

    own_local.wait()
    own_core.wait()
    for side in (0, 1):
        pl.when(unit_of(side, 1)[1])(lambda side=side: near_copy(side).wait())
    for d in range(1, chips):
        for k in range(pieces):
            for side in (0, 1):
                unit, valid, onward = unit_of(side, d)

                @pl.when(onward)
                def _():
                    z_copy(unit, side, d, k).wait_send()

                @pl.when(valid)
                def _():
                    x_copy(unit, side, d, k).wait_send()
                    c_copy(unit, side, d, k).wait()
                    cx_copy(unit, k).wait()


def gather_blocks(projector, left, right, tie):
    n_sec = lax.axis_size("sec")
    chips = n_sec // 2
    pieces = 4 if chips <= 4 else 1
    pair = pltpu.SemaphoreType.DMA((chips, pieces))
    return pl.pallas_call(
        functools.partial(gather_kernel, n_sec, pieces),
        out_shape=jax.ShapeDtypeStruct((n_sec,) + projector.shape, projector.dtype),
        in_specs=[pl.BlockSpec(memory_space=pl.ANY)] * 4,
        out_specs=pl.BlockSpec(memory_space=pl.ANY),
        scratch_shapes=[pltpu.SemaphoreType.DMA((3,))] + [pair] * 8,
        compiler_params=pltpu.CompilerParams(collective_id=0, has_side_effects=True),
        cost_estimate=pl.CostEstimate(
            flops=0, bytes_accessed=200_000_000, transcendentals=0
        ),
    )(projector, left, right, tie)


def clip_kernel(
    n_sec, n_tp, entries, delta_ref, out_ref,
    parts, norm_own, norms, scaled, far, part_send, part_recv,
    norm_send, norm_recv, far_sem, all_send, all_recv,
):
    pod = lax.axis_index("outer")
    sec = lax.axis_index("sec")
    tp = lax.axis_index("tp")
    barrier = pltpu.get_barrier_semaphore()
    peers = n_sec * n_tp
    me = tp * n_sec + sec

    def peer(j):
        other = lax.rem(me + j, peers)
        return (pod, other % n_sec, other // n_sec)

    for j in range(1, peers):
        pl.semaphore_signal(barrier, inc=1, device_id=peer(j), device_id_type=MESH)
    pl.semaphore_signal(barrier, inc=1, device_id=(1 - pod, sec, tp), device_id_type=MESH)
    pl.semaphore_wait(barrier, peers)

    def part_copy(j):
        to = lax.rem(sec + j, n_sec)
        return pltpu.make_async_remote_copy(
            src_ref=delta_ref.at[to], dst_ref=parts.at[j - 1],
            send_sem=part_send.at[j - 1], recv_sem=part_recv.at[j - 1],
            device_id=(pod, to, tp), device_id_type=MESH,
        )

    def norm_copy(j):
        return pltpu.make_async_remote_copy(
            src_ref=norm_own, dst_ref=norms.at[j - 1],
            send_sem=norm_send.at[j - 1], recv_sem=norm_recv.at[j - 1],
            device_id=peer(j), device_id_type=MESH,
        )

    def all_copy(j):
        to = lax.rem(sec + j, n_sec)
        return pltpu.make_async_remote_copy(
            src_ref=out_ref.at[sec], dst_ref=out_ref.at[sec],
            send_sem=all_send.at[j - 1], recv_sem=all_recv.at[j - 1],
            device_id=(pod, to, tp), device_id_type=MESH,
        )

    for j in range(1, n_sec):
        part_copy(j).start()
    total = delta_ref[sec]
    for j in range(1, n_sec):
        part_copy(j).wait_recv()
        total = total + parts[j - 1]
    norm_own[...] = jnp.broadcast_to(jnp.sum(total * total, keepdims=True), norm_own.shape)
    for j in range(1, peers):
        norm_copy(j).start()
    square = norm_own[...]
    for j in range(1, peers):
        norm_copy(j).wait_recv()
        square = square + norms[j - 1]
    factor = jnp.minimum(1.0, 1.0 / jnp.sqrt(square / entries + 1e-06))
    scaled[...] = total * factor[0:1, 0:1]
    across = pltpu.make_async_remote_copy(
        src_ref=scaled, dst_ref=far, send_sem=far_sem.at[0], recv_sem=far_sem.at[1],
        device_id=(1 - pod, sec, tp), device_id_type=MESH,
    )
    across.start()
    across.wait()
    out_ref[sec] = (scaled[...] + far[...]) * 0.5
    for j in range(1, n_sec):
        all_copy(j).start()
    for j in range(1, n_sec):
        all_copy(j).wait()
        part_copy(j).wait_send()
    for j in range(1, peers):
        norm_copy(j).wait_send()


def clipped_mean(local_delta):
    n_sec = lax.axis_size("sec")
    n_tp = lax.axis_size("tp")
    rows, width = local_delta.shape
    share = -(-rows // n_sec)
    stacked = jnp.pad(local_delta, ((0, share * n_sec - rows), (0, 0)))
    stacked = stacked.reshape(n_sec, share, width)
    shard = (share, width)
    dma = pltpu.SemaphoreType.DMA
    average = pl.pallas_call(
        functools.partial(clip_kernel, n_sec, n_tp, rows * width * n_tp),
        out_shape=jax.ShapeDtypeStruct(stacked.shape, jnp.float32),
        in_specs=[pl.BlockSpec(memory_space=pltpu.VMEM)],
        out_specs=pl.BlockSpec(memory_space=pltpu.VMEM),
        scratch_shapes=[
            pltpu.VMEM((n_sec - 1,) + shard, jnp.float32),
            pltpu.VMEM((8, 128), jnp.float32),
            pltpu.VMEM((n_sec * n_tp - 1, 8, 128), jnp.float32),
            pltpu.VMEM(shard, jnp.float32),
            pltpu.VMEM(shard, jnp.float32),
            dma((n_sec - 1,)),
            dma((n_sec - 1,)),
            dma((n_sec * n_tp - 1,)),
            dma((n_sec * n_tp - 1,)),
            dma((2,)),
            dma((n_sec - 1,)),
            dma((n_sec - 1,)),
        ],
        compiler_params=pltpu.CompilerParams(
            collective_id=1, has_side_effects=True, vmem_limit_bytes=24 * 1024 * 1024
        ),
    )(stacked)
    return average.reshape(n_sec * share, width)[:rows]


def shape_mask(tile_shape, grid):
    places = lax.broadcasted_iota(jnp.int32, (1, grid), 1)
    rows_ok = places < tile_shape[:, 0:1]
    cols_ok = places < tile_shape[:, 1:2]
    return (rows_ok[:, :, None] & cols_ok[:, None, :]).astype(jnp.float32)


def on_device(
    tile_maps,
    tile_shape,
    conv_kernel,
    norm_gain,
    norm_bias,
    projector,
    text_rows,
    row_order,
    seq_gain,
    cotangent,
):
    grid = tile_maps.shape[1]
    half_ch = tile_maps.shape[3]
    channels = half_ch * lax.axis_size("tp")
    rows_dev = tile_maps.shape[0] * grid * grid
    width = text_rows.shape[1] * lax.axis_size("tp")
    n_sec = lax.axis_size("sec")
    half_rows = projector.shape[0] // 2
    first_half = lax.dynamic_slice_in_dim(
        projector, lax.axis_index("outer") * half_rows, half_rows, axis=0
    )
    from_left = lax.ppermute(first_half, "sec", [(i, i + 2) for i in range(n_sec - 2)])
    from_right = lax.ppermute(first_half, "sec", [(i + 2, i) for i in range(n_sec - 2)])
    validity = shape_mask(tile_shape, grid)[..., None]
    masked = tile_maps.astype(jnp.float32) * validity
    padded = jnp.pad(masked, ((0, 0), (3, 3), (3, 3), (0, 0)))
    conv_out = jnp.zeros(masked.shape, jnp.float32)
    for row_off in range(7):
        for col_off in range(7):
            conv_out = (
                conv_out
                + padded[:, row_off : row_off + grid, col_off : col_off + grid, :]
                * conv_kernel[row_off, col_off]
            )
    total_one, total_two = lax.psum(
        (jnp.sum(conv_out, axis=-1), jnp.sum(conv_out * conv_out, axis=-1)), "tp"
    )
    center = (total_one / channels)[..., None]
    inverse = lax.rsqrt((total_two / channels)[..., None] - center * center + 1e-06)
    normal = (conv_out - center) * inverse
    features = (
        (validity * (normal * norm_gain + norm_bias))
        .astype(jnp.bfloat16)
        .reshape(rows_dev, half_ch)
    )
    tp_size = lax.axis_size("tp")
    half_width = text_rows.shape[1]
    mine = lax.axis_index("tp")
    swap = [(i, (i + 1) % tp_size) for i in range(tp_size)]
    gathered = gather_blocks(projector, from_left, from_right, features)
    per_half = gathered.shape[0] // tp_size
    own_weight = lax.dynamic_slice_in_dim(gathered, mine * per_half, per_half, axis=0)
    far_weight = lax.dynamic_slice_in_dim(gathered, (1 - mine) * per_half, per_half, axis=0)
    routed = lax.all_to_all(features, "sec", split_axis=0, concat_axis=0, tiled=True)

    def project(rows, weight):
        return jnp.concatenate(
            [
                jnp.dot(rows, weight[block], preferred_element_type=jnp.float32)
                for block in range(per_half)
            ],
            axis=1,
        )

    sent = project(routed, far_weight).astype(jnp.bfloat16)
    other = lax.ppermute(sent, "tp", swap)
    arrived = (project(routed, own_weight) + other.astype(jnp.float32)).astype(jnp.bfloat16)
    positions = row_order[0, :rows_dev]
    merged = text_rows.at[positions].set(arrived)
    wide = merged.astype(jnp.float32)
    upstream = cotangent.astype(jnp.float32) * seq_gain
    square_sum, along = lax.psum(
        (jnp.sum(wide * wide, axis=-1), jnp.sum(upstream * wide, axis=-1)), "tp"
    )
    inv_rms = lax.rsqrt(square_sum / width + 1e-05)[:, None]
    normed = (wide * inv_rms * seq_gain).astype(jnp.bfloat16)
    grad_seq = inv_rms * upstream - wide * (inv_rms * inv_rms * inv_rms) * along[:, None] / width
    picked = grad_seq[positions].astype(jnp.bfloat16)
    far_picked = lax.ppermute(picked, "tp", swap)

    def project_back(rows, weight):
        step = weight.shape[2]
        total = jnp.zeros((rows.shape[0], half_ch), jnp.float32)
        for block in range(per_half):
            total = total + lax.dot_general(
                rows[:, block * step : (block + 1) * step],
                weight[block],
                (((1,), (1,)), ((), ())),
                preferred_element_type=jnp.float32,
            )
        return total

    back = (project_back(picked, own_weight) + project_back(far_picked, far_weight)).astype(
        jnp.bfloat16
    )
    grad_rows = lax.all_to_all(back, "sec", split_axis=0, concat_axis=0, tiled=True).astype(
        jnp.float32
    )
    masked_grad = grad_rows.reshape(masked.shape) * validity
    scaled = masked_grad * norm_gain
    first_sum, second_sum = lax.psum(
        (jnp.sum(scaled, axis=-1), jnp.sum(scaled * normal, axis=-1)), "tp"
    )
    grad_conv = inverse * (
        scaled - (first_sum / channels)[..., None] - normal * (second_sum / channels)[..., None]
    )
    kernel_rows = []
    for row_off in range(7):
        for col_off in range(7):
            window = padded[:, row_off : row_off + grid, col_off : col_off + grid, :]
            kernel_rows.append(jnp.sum(window * grad_conv, axis=(0, 1, 2)))
    gain_grad = jnp.sum(masked_grad * normal, axis=(0, 1, 2))
    bias_grad = jnp.sum(masked_grad, axis=(0, 1, 2))
    local_delta = jnp.stack(kernel_rows + [gain_grad, bias_grad], axis=0)
    average = clipped_mean(local_delta)
    return (normed, average[:49].reshape(7, 7, half_ch), average[49], average[50])


def solution(mesh):
    in_specs = (
        P(("outer", "sec"), None, None, "tp"),
        P(("outer", "sec"), None),
        P(None, None, "tp"),
        P("tp"),
        P("tp"),
        P("tp", "sec"),
        P(("outer", "sec"), "tp"),
        P(("outer", "sec"), None),
        P("tp"),
        P(("outer", "sec"), "tp"),
    )
    out_specs = (P(("outer", "sec"), "tp"), P(None, None, "tp"), P("tp"), P("tp"))
    return jax.shard_map(
        on_device, mesh=mesh, in_specs=in_specs, out_specs=out_specs, check_vma=False
    )
```

```python
import jax
import jax.numpy as jnp
from jax import lax
from jax.experimental import pallas as pl
from jax.experimental.pallas import tpu as pltpu
from jax.sharding import PartitionSpec as P
import functools

MESH = pl.DeviceIdType.MESH


def clip_kernel(
    n_sec, n_tp, entries, delta_ref, out_ref,
    parts, norm_own, norms, scaled, far, part_send, part_recv,
    norm_send, norm_recv, far_sem, all_send, all_recv,
):
    pod = lax.axis_index("outer")
    sec = lax.axis_index("sec")
    tp = lax.axis_index("tp")
    barrier = pltpu.get_barrier_semaphore()
    peers = n_sec * n_tp
    me = tp * n_sec + sec

    def peer(j):
        other = lax.rem(me + j, peers)
        return (pod, other % n_sec, other // n_sec)

    for j in range(1, peers):
        pl.semaphore_signal(barrier, inc=1, device_id=peer(j), device_id_type=MESH)
    pl.semaphore_signal(barrier, inc=1, device_id=(1 - pod, sec, tp), device_id_type=MESH)
    pl.semaphore_wait(barrier, peers)

    def part_copy(j):
        to = lax.rem(sec + j, n_sec)
        return pltpu.make_async_remote_copy(
            src_ref=delta_ref.at[to], dst_ref=parts.at[j - 1],
            send_sem=part_send.at[j - 1], recv_sem=part_recv.at[j - 1],
            device_id=(pod, to, tp), device_id_type=MESH,
        )

    def norm_copy(j):
        return pltpu.make_async_remote_copy(
            src_ref=norm_own, dst_ref=norms.at[j - 1],
            send_sem=norm_send.at[j - 1], recv_sem=norm_recv.at[j - 1],
            device_id=peer(j), device_id_type=MESH,
        )

    def all_copy(j):
        to = lax.rem(sec + j, n_sec)
        return pltpu.make_async_remote_copy(
            src_ref=out_ref.at[sec], dst_ref=out_ref.at[sec],
            send_sem=all_send.at[j - 1], recv_sem=all_recv.at[j - 1],
            device_id=(pod, to, tp), device_id_type=MESH,
        )

    for j in range(1, n_sec):
        part_copy(j).start()
    total = delta_ref[sec]
    for j in range(1, n_sec):
        part_copy(j).wait_recv()
        total = total + parts[j - 1]
    norm_own[...] = jnp.broadcast_to(jnp.sum(total * total, keepdims=True), norm_own.shape)
    for j in range(1, peers):
        norm_copy(j).start()
    square = norm_own[...]
    for j in range(1, peers):
        norm_copy(j).wait_recv()
        square = square + norms[j - 1]
    factor = jnp.minimum(1.0, 1.0 / jnp.sqrt(square / entries + 1e-06))
    scaled[...] = total * factor[0:1, 0:1]
    across = pltpu.make_async_remote_copy(
        src_ref=scaled, dst_ref=far, send_sem=far_sem.at[0], recv_sem=far_sem.at[1],
        device_id=(1 - pod, sec, tp), device_id_type=MESH,
    )
    across.start()
    across.wait()
    out_ref[sec] = (scaled[...] + far[...]) * 0.5
    for j in range(1, n_sec):
        all_copy(j).start()
    for j in range(1, n_sec):
        all_copy(j).wait()
        part_copy(j).wait_send()
    for j in range(1, peers):
        norm_copy(j).wait_send()


def clipped_mean(local_delta):
    n_sec = lax.axis_size("sec")
    n_tp = lax.axis_size("tp")
    rows, width = local_delta.shape
    share = -(-rows // n_sec)
    stacked = jnp.pad(local_delta, ((0, share * n_sec - rows), (0, 0)))
    stacked = stacked.reshape(n_sec, share, width)
    shard = (share, width)
    dma = pltpu.SemaphoreType.DMA
    average = pl.pallas_call(
        functools.partial(clip_kernel, n_sec, n_tp, rows * width * n_tp),
        out_shape=jax.ShapeDtypeStruct(stacked.shape, jnp.float32),
        in_specs=[pl.BlockSpec(memory_space=pltpu.VMEM)],
        out_specs=pl.BlockSpec(memory_space=pltpu.VMEM),
        scratch_shapes=[
            pltpu.VMEM((n_sec - 1,) + shard, jnp.float32),
            pltpu.VMEM((8, 128), jnp.float32),
            pltpu.VMEM((n_sec * n_tp - 1, 8, 128), jnp.float32),
            pltpu.VMEM(shard, jnp.float32),
            pltpu.VMEM(shard, jnp.float32),
            dma((n_sec - 1,)),
            dma((n_sec - 1,)),
            dma((n_sec * n_tp - 1,)),
            dma((n_sec * n_tp - 1,)),
            dma((2,)),
            dma((n_sec - 1,)),
            dma((n_sec - 1,)),
        ],
        compiler_params=pltpu.CompilerParams(
            collective_id=1, has_side_effects=True, vmem_limit_bytes=24 * 1024 * 1024
        ),
    )(stacked)
    return average.reshape(n_sec * share, width)[:rows]


def shape_mask(tile_shape, grid):
    places = lax.broadcasted_iota(jnp.int32, (1, grid), 1)
    rows_ok = places < tile_shape[:, 0:1]
    cols_ok = places < tile_shape[:, 1:2]
    return (rows_ok[:, :, None] & cols_ok[:, None, :]).astype(jnp.float32)


def on_device(
    tile_maps,
    tile_shape,
    conv_kernel,
    norm_gain,
    norm_bias,
    projector,
    text_rows,
    row_order,
    seq_gain,
    cotangent,
):
    grid = tile_maps.shape[1]
    half_ch = tile_maps.shape[3]
    channels = half_ch * lax.axis_size("tp")
    rows_dev = tile_maps.shape[0] * grid * grid
    width = text_rows.shape[1] * lax.axis_size("tp")
    positions = row_order[0, :rows_dev]
    cut = (projector.shape[1] // 2 + 127) // 128 * 128
    near_cols = lax.all_gather(projector[:, :cut], "sec", axis=0, tiled=False)
    rest_cols = lax.all_gather(projector[:, cut:], "sec", axis=0, tiled=False)
    validity = shape_mask(tile_shape, grid)[..., None]
    masked = tile_maps.astype(jnp.float32) * validity
    padded = jnp.pad(masked, ((0, 0), (3, 3), (3, 3), (0, 0)))
    conv_out = jnp.zeros(masked.shape, jnp.float32)
    for row_off in range(7):
        for col_off in range(7):
            conv_out = (
                conv_out
                + padded[:, row_off : row_off + grid, col_off : col_off + grid, :]
                * conv_kernel[row_off, col_off]
            )
    text_wide = text_rows.astype(jnp.float32)
    total_one, total_two, text_square = lax.psum(
        (
            jnp.sum(conv_out, axis=-1),
            jnp.sum(conv_out * conv_out, axis=-1),
            jnp.sum(text_wide * text_wide, axis=-1),
        ),
        "tp",
    )
    center = (total_one / channels)[..., None]
    inverse = lax.rsqrt((total_two / channels)[..., None] - center * center + 1e-06)
    normal = (conv_out - center) * inverse
    features = (
        (validity * (normal * norm_gain + norm_bias))
        .astype(jnp.bfloat16)
        .reshape(rows_dev, half_ch)
    )
    tp_size = lax.axis_size("tp")
    half_width = text_rows.shape[1]
    mine = lax.axis_index("tp")
    swap = [(i, (i + 1) % tp_size) for i in range(tp_size)]
    per_half = near_cols.shape[0] // tp_size

    def halves(weight):
        own = lax.dynamic_slice_in_dim(weight, mine * per_half, per_half, axis=0)
        far = lax.dynamic_slice_in_dim(weight, (1 - mine) * per_half, per_half, axis=0)
        return own, far

    own_near, far_near = halves(near_cols)
    own_rest, far_rest = halves(rest_cols)
    routed = lax.all_to_all(features, "sec", split_axis=0, concat_axis=0, tiled=True)

    def project(rows, weight):
        return [
            jnp.dot(rows, weight[block], preferred_element_type=jnp.float32)
            for block in range(per_half)
        ]

    def summed(own, far):
        sent = jnp.concatenate(
            [part.astype(jnp.bfloat16) for part in project(routed, far)], axis=1
        )
        other = lax.ppermute(sent, "tp", swap)
        step = own.shape[2]
        return [
            (part + other[:, k * step : (k + 1) * step].astype(jnp.float32)).astype(jnp.bfloat16)
            for k, part in enumerate(project(routed, own))
        ]

    near_parts = summed(own_near, far_near)
    rest_parts = summed(own_rest, far_rest)
    arrived = jnp.concatenate(
        [part for pair in zip(near_parts, rest_parts) for part in pair], axis=1
    )
    placed_cotangent = lax.optimization_barrier(cotangent[positions])
    wide = arrived.astype(jnp.float32)
    upstream = placed_cotangent.astype(jnp.float32) * seq_gain
    square_sum, along = lax.psum(
        (jnp.sum(wide * wide, axis=-1), jnp.sum(upstream * wide, axis=-1)), "tp"
    )
    inv_rms = lax.rsqrt(square_sum / width + 1e-05)
    inv_col = inv_rms[:, None]
    picked = (
        inv_col * upstream - wide * (inv_col * inv_col * inv_col) * along[:, None] / width
    ).astype(jnp.bfloat16)
    merged = text_rows.at[positions].set(arrived)
    inv_all = lax.rsqrt(text_square / width + 1e-05).at[positions].set(inv_rms)
    normed = (merged.astype(jnp.float32) * inv_all[:, None] * seq_gain).astype(jnp.bfloat16)
    middle = per_half // 2 * projector.shape[1]
    far_first = lax.ppermute(picked[:, :middle], "tp", swap)
    far_second = lax.ppermute(picked[:, middle:], "tp", swap)

    def project_back(rows, near, rest, first):
        block_width = projector.shape[1]
        total = jnp.zeros((rows.shape[0], half_ch), jnp.float32)
        for k in range(rows.shape[1] // block_width):
            start = k * block_width
            for weight, low, high in (
                (near, start, start + cut),
                (rest, start + cut, start + block_width),
            ):
                total = total + lax.dot_general(
                    rows[:, low:high],
                    weight[first + k],
                    (((1,), (1,)), ((), ())),
                    preferred_element_type=jnp.float32,
                )
        return total

    back = (
        project_back(picked, own_near, own_rest, 0)
        + project_back(far_first, far_near, far_rest, 0)
        + project_back(far_second, far_near, far_rest, per_half // 2)
    ).astype(jnp.bfloat16)
    grad_rows = lax.all_to_all(back, "sec", split_axis=0, concat_axis=0, tiled=True).astype(
        jnp.float32
    )
    masked_grad = grad_rows.reshape(masked.shape) * validity
    scaled = masked_grad * norm_gain
    first_sum, second_sum = lax.psum(
        (jnp.sum(scaled, axis=-1), jnp.sum(scaled * normal, axis=-1)), "tp"
    )
    grad_conv = inverse * (
        scaled - (first_sum / channels)[..., None] - normal * (second_sum / channels)[..., None]
    )
    kernel_rows = []
    for row_off in range(7):
        for col_off in range(7):
            window = padded[:, row_off : row_off + grid, col_off : col_off + grid, :]
            kernel_rows.append(jnp.sum(window * grad_conv, axis=(0, 1, 2)))
    gain_grad = jnp.sum(masked_grad * normal, axis=(0, 1, 2))
    bias_grad = jnp.sum(masked_grad, axis=(0, 1, 2))
    local_delta = jnp.stack(kernel_rows + [gain_grad, bias_grad], axis=0)
    average = clipped_mean(local_delta)
    return (normed, average[:49].reshape(7, 7, half_ch), average[49], average[50])


def solution(mesh):
    in_specs = (
        P(("outer", "sec"), None, None, "tp"),
        P(("outer", "sec"), None),
        P(None, None, "tp"),
        P("tp"),
        P("tp"),
        P("tp", "sec"),
        P(("outer", "sec"), "tp"),
        P(("outer", "sec"), None),
        P("tp"),
        P(("outer", "sec"), "tp"),
    )
    out_specs = (P(("outer", "sec"), "tp"), P(None, None, "tp"), P("tp"), P("tp"))
    return jax.shard_map(
        on_device, mesh=mesh, in_specs=in_specs, out_specs=out_specs, check_vma=False
    )
```

```python
import jax
import jax.numpy as jnp
from jax import lax
from jax.experimental import pallas as pl
from jax.experimental.pallas import tpu as pltpu
from jax.sharding import PartitionSpec as P
import functools

MESH = pl.DeviceIdType.MESH


def clip_kernel(
    n_sec, n_tp, entries, delta_ref, out_ref,
    parts, norm_own, norms, scaled, far, part_send, part_recv,
    norm_send, norm_recv, far_sem, all_send, all_recv,
):
    pod = lax.axis_index("outer")
    sec = lax.axis_index("sec")
    tp = lax.axis_index("tp")
    barrier = pltpu.get_barrier_semaphore()
    peers = n_sec * n_tp
    me = tp * n_sec + sec

    def peer(j):
        other = lax.rem(me + j, peers)
        return (pod, other % n_sec, other // n_sec)

    for j in range(1, peers):
        pl.semaphore_signal(barrier, inc=1, device_id=peer(j), device_id_type=MESH)
    pl.semaphore_signal(barrier, inc=1, device_id=(1 - pod, sec, tp), device_id_type=MESH)
    pl.semaphore_wait(barrier, peers)

    def part_copy(j):
        to = lax.rem(sec + j, n_sec)
        return pltpu.make_async_remote_copy(
            src_ref=delta_ref.at[to], dst_ref=parts.at[j - 1],
            send_sem=part_send.at[j - 1], recv_sem=part_recv.at[j - 1],
            device_id=(pod, to, tp), device_id_type=MESH,
        )

    def norm_copy(j):
        return pltpu.make_async_remote_copy(
            src_ref=norm_own, dst_ref=norms.at[j - 1],
            send_sem=norm_send.at[j - 1], recv_sem=norm_recv.at[j - 1],
            device_id=peer(j), device_id_type=MESH,
        )

    def all_copy(j):
        to = lax.rem(sec + j, n_sec)
        return pltpu.make_async_remote_copy(
            src_ref=out_ref.at[sec], dst_ref=out_ref.at[sec],
            send_sem=all_send.at[j - 1], recv_sem=all_recv.at[j - 1],
            device_id=(pod, to, tp), device_id_type=MESH,
        )

    for j in range(1, n_sec):
        part_copy(j).start()
    total = delta_ref[sec]
    for j in range(1, n_sec):
        part_copy(j).wait_recv()
        total = total + parts[j - 1]
    norm_own[...] = jnp.broadcast_to(jnp.sum(total * total, keepdims=True), norm_own.shape)
    for j in range(1, peers):
        norm_copy(j).start()
    square = norm_own[...]
    for j in range(1, peers):
        norm_copy(j).wait_recv()
        square = square + norms[j - 1]
    factor = jnp.minimum(1.0, 1.0 / jnp.sqrt(square / entries + 1e-06))
    scaled[...] = total * factor[0:1, 0:1]
    across = pltpu.make_async_remote_copy(
        src_ref=scaled, dst_ref=far, send_sem=far_sem.at[0], recv_sem=far_sem.at[1],
        device_id=(1 - pod, sec, tp), device_id_type=MESH,
    )
    across.start()
    across.wait()
    out_ref[sec] = (scaled[...] + far[...]) * 0.5
    for j in range(1, n_sec):
        all_copy(j).start()
    for j in range(1, n_sec):
        all_copy(j).wait()
        part_copy(j).wait_send()
    for j in range(1, peers):
        norm_copy(j).wait_send()


def clipped_mean(local_delta):
    n_sec = lax.axis_size("sec")
    n_tp = lax.axis_size("tp")
    rows, width = local_delta.shape
    share = -(-rows // n_sec)
    stacked = jnp.pad(local_delta, ((0, share * n_sec - rows), (0, 0)))
    stacked = stacked.reshape(n_sec, share, width)
    shard = (share, width)
    dma = pltpu.SemaphoreType.DMA
    average = pl.pallas_call(
        functools.partial(clip_kernel, n_sec, n_tp, rows * width * n_tp),
        out_shape=jax.ShapeDtypeStruct(stacked.shape, jnp.float32),
        in_specs=[pl.BlockSpec(memory_space=pltpu.VMEM)],
        out_specs=pl.BlockSpec(memory_space=pltpu.VMEM),
        scratch_shapes=[
            pltpu.VMEM((n_sec - 1,) + shard, jnp.float32),
            pltpu.VMEM((8, 128), jnp.float32),
            pltpu.VMEM((n_sec * n_tp - 1, 8, 128), jnp.float32),
            pltpu.VMEM(shard, jnp.float32),
            pltpu.VMEM(shard, jnp.float32),
            dma((n_sec - 1,)),
            dma((n_sec - 1,)),
            dma((n_sec * n_tp - 1,)),
            dma((n_sec * n_tp - 1,)),
            dma((2,)),
            dma((n_sec - 1,)),
            dma((n_sec - 1,)),
        ],
        compiler_params=pltpu.CompilerParams(
            collective_id=1, has_side_effects=True, vmem_limit_bytes=24 * 1024 * 1024
        ),
    )(stacked)
    return average.reshape(n_sec * share, width)[:rows]


def shape_mask(tile_shape, grid):
    places = lax.broadcasted_iota(jnp.int32, (1, grid), 1)
    rows_ok = places < tile_shape[:, 0:1]
    cols_ok = places < tile_shape[:, 1:2]
    return (rows_ok[:, :, None] & cols_ok[:, None, :]).astype(jnp.float32)


def on_device(
    tile_maps,
    tile_shape,
    conv_kernel,
    norm_gain,
    norm_bias,
    projector,
    text_rows,
    row_order,
    seq_gain,
    cotangent,
):
    grid = tile_maps.shape[1]
    half_ch = tile_maps.shape[3]
    channels = half_ch * lax.axis_size("tp")
    rows_dev = tile_maps.shape[0] * grid * grid
    width = text_rows.shape[1] * lax.axis_size("tp")
    positions = row_order[0, :rows_dev]
    cut = max(128, projector.shape[1] * 2 // 7 // 128 * 128)
    near_cols = lax.all_gather(projector[:, :cut], "sec", axis=0, tiled=False)
    rest_cols = lax.all_gather(projector[:, cut:], "sec", axis=0, tiled=False)
    validity = shape_mask(tile_shape, grid)[..., None]
    masked = tile_maps.astype(jnp.float32) * validity
    padded = jnp.pad(masked, ((0, 0), (3, 3), (3, 3), (0, 0)))
    conv_out = jnp.zeros(masked.shape, jnp.float32)
    for row_off in range(7):
        for col_off in range(7):
            conv_out = (
                conv_out
                + padded[:, row_off : row_off + grid, col_off : col_off + grid, :]
                * conv_kernel[row_off, col_off]
            )
    text_wide = text_rows.astype(jnp.float32)
    total_one, total_two, text_square = lax.psum(
        (
            jnp.sum(conv_out, axis=-1),
            jnp.sum(conv_out * conv_out, axis=-1),
            jnp.sum(text_wide * text_wide, axis=-1),
        ),
        "tp",
    )
    center = (total_one / channels)[..., None]
    inverse = lax.rsqrt((total_two / channels)[..., None] - center * center + 1e-06)
    normal = (conv_out - center) * inverse
    features = (
        (validity * (normal * norm_gain + norm_bias))
        .astype(jnp.bfloat16)
        .reshape(rows_dev, half_ch)
    )
    tp_size = lax.axis_size("tp")
    half_width = text_rows.shape[1]
    mine = lax.axis_index("tp")
    features, text_square = lax.optimization_barrier((features, text_square))
    swap = [(i, (i + 1) % tp_size) for i in range(tp_size)]
    per_half = near_cols.shape[0] // tp_size

    def halves(weight):
        own = lax.dynamic_slice_in_dim(weight, mine * per_half, per_half, axis=0)
        far = lax.dynamic_slice_in_dim(weight, (1 - mine) * per_half, per_half, axis=0)
        return own, far

    own_rest, far_rest = halves(rest_cols)
    routed = lax.all_to_all(features, "sec", split_axis=0, concat_axis=0, tiled=True)

    def project(rows, weight):
        return [
            jnp.dot(rows, weight[block], preferred_element_type=jnp.float32)
            for block in range(per_half)
        ]

    def summed(routed, own, far):
        sent = jnp.concatenate(
            [part.astype(jnp.bfloat16) for part in project(routed, far)], axis=1
        )
        other = lax.ppermute(sent, "tp", swap)
        step = own.shape[2]
        return [
            (part + other[:, k * step : (k + 1) * step].astype(jnp.float32)).astype(jnp.bfloat16)
            for k, part in enumerate(project(routed, own))
        ]

    rest_parts = summed(routed, own_rest, far_rest)
    rest_parts, routed_later, near_cols = lax.optimization_barrier(
        (rest_parts, routed, near_cols)
    )
    own_near, far_near = halves(near_cols)
    near_parts = summed(routed_later, own_near, far_near)
    arrived = jnp.concatenate(
        [part for pair in zip(near_parts, rest_parts) for part in pair], axis=1
    )
    placed_cotangent = lax.optimization_barrier(cotangent[positions])
    wide = arrived.astype(jnp.float32)
    upstream = placed_cotangent.astype(jnp.float32) * seq_gain
    square_sum, along = lax.psum(
        (jnp.sum(wide * wide, axis=-1), jnp.sum(upstream * wide, axis=-1)), "tp"
    )
    inv_rms = lax.rsqrt(square_sum / width + 1e-05)
    inv_col = inv_rms[:, None]
    picked = (
        inv_col * upstream - wide * (inv_col * inv_col * inv_col) * along[:, None] / width
    ).astype(jnp.bfloat16)
    merged = text_rows.at[positions].set(arrived)
    inv_all = lax.rsqrt(text_square / width + 1e-05).at[positions].set(inv_rms)
    normed = (merged.astype(jnp.float32) * inv_all[:, None] * seq_gain).astype(jnp.bfloat16)
    middle = per_half // 2 * projector.shape[1]
    far_first = lax.ppermute(picked[:, :middle], "tp", swap)
    far_second = lax.ppermute(picked[:, middle:], "tp", swap)

    def project_back(rows, near, rest, first):
        block_width = projector.shape[1]
        total = jnp.zeros((rows.shape[0], half_ch), jnp.float32)
        for k in range(rows.shape[1] // block_width):
            start = k * block_width
            for weight, low, high in (
                (near, start, start + cut),
                (rest, start + cut, start + block_width),
            ):
                total = total + lax.dot_general(
                    rows[:, low:high],
                    weight[first + k],
                    (((1,), (1,)), ((), ())),
                    preferred_element_type=jnp.float32,
                )
        return total

    back = (
        project_back(picked, own_near, own_rest, 0)
        + project_back(far_first, far_near, far_rest, 0)
        + project_back(far_second, far_near, far_rest, per_half // 2)
    ).astype(jnp.bfloat16)
    grad_rows = lax.all_to_all(back, "sec", split_axis=0, concat_axis=0, tiled=True).astype(
        jnp.float32
    )
    masked_grad = grad_rows.reshape(masked.shape) * validity
    scaled = masked_grad * norm_gain
    first_sum, second_sum = lax.psum(
        (jnp.sum(scaled, axis=-1), jnp.sum(scaled * normal, axis=-1)), "tp"
    )
    grad_conv = inverse * (
        scaled - (first_sum / channels)[..., None] - normal * (second_sum / channels)[..., None]
    )
    kernel_rows = []
    for row_off in range(7):
        for col_off in range(7):
            window = padded[:, row_off : row_off + grid, col_off : col_off + grid, :]
            kernel_rows.append(jnp.sum(window * grad_conv, axis=(0, 1, 2)))
    gain_grad = jnp.sum(masked_grad * normal, axis=(0, 1, 2))
    bias_grad = jnp.sum(masked_grad, axis=(0, 1, 2))
    local_delta = jnp.stack(kernel_rows + [gain_grad, bias_grad], axis=0)
    average = clipped_mean(local_delta)
    return (normed, average[:49].reshape(7, 7, half_ch), average[49], average[50])


def solution(mesh):
    in_specs = (
        P(("outer", "sec"), None, None, "tp"),
        P(("outer", "sec"), None),
        P(None, None, "tp"),
        P("tp"),
        P("tp"),
        P("tp", "sec"),
        P(("outer", "sec"), "tp"),
        P(("outer", "sec"), None),
        P("tp"),
        P(("outer", "sec"), "tp"),
    )
    out_specs = (P(("outer", "sec"), "tp"), P(None, None, "tp"), P("tp"), P("tp"))
    return jax.shard_map(
        on_device, mesh=mesh, in_specs=in_specs, out_specs=out_specs, check_vma=False
    )
```
